512 devices in a mesh: img: 32 (over z_hi, y, core), blk: 16 (over z_lo, x).
Axes of the slice: x: 4, y: 8, z: 8 (z_hi: 2, z_lo: 4; z = z_hi * 4 + z_lo), core: 2. Of those that a mesh axis runs over, the one named last changes fastest.
Arguments:
- images: bfloat16 [10240, 2, 20480], P('img', None, 'blk'), may hold values from -70 to 70
- projections: bfloat16 [192, 2, 20480], P(None, None, 'blk'), may hold values from -6 to 6
- ctf_table: float32 [16, 20480], P(None, 'blk'), may hold values from -1 to 1
- ctf_group: int32 [10240], P('img'), may hold values from 0 to 15
- noise_weight: float32 [20480], P('blk'), may hold values from 0.002 to 0.02
- significant: int32 [10240, 48], P('img'), may hold values from 0 to 191, all different within a row
Outputs:
- slices: float32 [192, 2, 20480], P('img', None, 'blk')
- spectrum: float32 [20480], P('blk')
The draws below stay inside these ranges and needn't reach their ends.
Inputs may be any that keep to these rules, and one draw needn't show every extreme that they name: `significant`: the 48 entries of each row are different orientations.
All inputs are finite; a program needn't handle non-finite values.
Results may differ from the reference program's by a relative error of at most 0.0019.
The reference program's roundings to bfloat16 on the way (of `left`, `power`, `right`, `weights` and `corrected`) count: a program that leaves them out, or rounds other values in their place, can miss the bound.
Values may be sent and summed in bfloat16 or wider, within the bound.
No kernel may reach another device: no remote copies, remote signals or barrier semaphores. Data moves between devices by JAX's collectives and lax.ppermute only.
A program may use at most 64 MiB of HBM per device.

```python
import math
import jax
import jax.numpy as jnp
from jax import lax

K = 20480
IMG_DEV = 320
SIG = 48
GROUPS = 16
IMAGES = 10240
ORIENT = 192
N_IMG = 32


def draw_images(key, part):
    key = jax.random.fold_in(key, 11)
    values = jax.random.truncated_normal(key, -6.0, 6.0, (IMAGES, 2, K), jnp.float32)
    return values.astype(jnp.bfloat16)


def set_ends(values, own_key, low, top_value):
    shape = values.shape
    spot = [jax.random.randint(jax.random.fold_in(own_key, axis), (), 0, shape[axis]) for axis in range(len(shape))]
    values = values.at[tuple(spot)].set(low)
    longest = shape.index(max(shape))
    spot[longest] = (spot[longest] + 1) % shape[longest]
    return values.at[tuple(spot)].set(top_value)


def block_levels(stream_key, extent, pieces, low, largest):
    loudness = 1.0
    for dim, blocks in pieces:
        steps = jax.random.uniform(jax.random.fold_in(jax.random.fold_in(stream_key, 6), dim), (blocks,), jnp.float32, low / len(pieces), largest / len(pieces))
        loudness = loudness * jnp.repeat(jnp.exp(steps), extent[dim] // blocks).reshape((-1,) + (1,) * (len(extent) - 1 - dim))
    return loudness


def different_ones(own_key, rows, amount, top, lift):
    order = jax.random.permutation(jax.random.fold_in(own_key, 1), amount)
    pull = order
    for power in range(3):
        pull = pull * pull // amount
    pull = pull * lift // amount
    tickets = jax.random.randint(jax.random.fold_in(own_key, 2), (rows, amount), 0, 4096) + pull
    fixed_rows = jax.random.permutation(jax.random.fold_in(own_key, 3), rows)[jnp.arange(amount) % rows]
    tickets = jnp.where(jnp.arange(rows)[:, None] == fixed_rows[None, :], 1 << 14, tickets)
    merit = tickets * amount + jnp.arange(amount)
    return lax.top_k(merit.astype(jnp.int32), top)[1].astype(jnp.int32)


def scatter_about(rng, extent, deviation, bound, pieces=(), kind=jnp.bfloat16):
    loudness = block_levels(rng, extent, pieces, -0.22, 0.18) if pieces else 1.0
    entries = jax.random.normal(rng, extent, jnp.float32) * deviation * loudness
    return jnp.minimum(jnp.maximum(entries, -bound), bound).astype(kind)


def setup_inputs(seed: int = 0) -> dict:
    key_list = jax.random.split(jax.random.key(seed), 7)
    return {
        "images": draw_images(jax.random.fold_in(key_list[6], 71), 0),
        "projections": scatter_about(key_list[1], (ORIENT, 2, K), 1.0, 6.0, ((2, 16),)),
        "ctf_table": jnp.clip(jax.random.uniform(key_list[2], (GROUPS, K), jnp.float32, -1.0, 1.0) * block_levels(key_list[2], (GROUPS, K), ((1, 16),), -0.4, 0.0), -1.0, 1.0),
        "ctf_group": set_ends(jax.random.randint(key_list[3], (IMAGES,), 0, GROUPS), jax.random.fold_in(key_list[3], 1), 0, GROUPS - 1).astype(jnp.int32),
        "noise_weight": jnp.clip(jnp.exp(math.log(0.02) - 2.30258502 * jax.random.uniform(key_list[4], (K,), jnp.float32) ** block_levels(key_list[4], (K,), ((0, 16),), -0.2, 0.2)), 0.002, 0.02),
        "significant": different_ones(key_list[5], IMAGES, ORIENT, SIG, 4096),
    }


def weights_of(scores, sig_rows):
    rows = jnp.arange(scores.shape[0], dtype=jnp.int32)[:, None]
    mask = jnp.zeros(scores.shape, jnp.float32).at[rows, sig_rows].set(1.0)
    top = jnp.max(jnp.where(mask > 0, scores, -jnp.inf), axis=1, keepdims=True)
    expo = jnp.exp(jnp.where(mask > 0, scores - top, -jnp.inf))
    return (expo / jnp.sum(expo, axis=1, keepdims=True)).astype(jnp.bfloat16)


def reference(images, projections, ctf_table, ctf_group, noise_weight, significant):
    pf = projections.astype(jnp.float32)
    power = (pf[:, 0] * pf[:, 0] + pf[:, 1] * pf[:, 1]).astype(jnp.bfloat16)
    right = jnp.concatenate([projections, power[:, None, :]], axis=1).reshape(ORIENT, 3 * K)
    img_blocks = images.reshape(N_IMG, IMG_DEV, 2, K)
    grp_blocks = ctf_group.reshape(N_IMG, IMG_DEV)
    sig_blocks = significant.reshape(N_IMG, IMG_DEV, SIG)

    def step(carry, block):
        acc_slices, acc_noise = carry
        imgs, grp, sig_rows = block
        ctf = ctf_table[grp]
        xf = imgs.astype(jnp.float32)
        scaled = ctf * noise_weight[None, :]
        left = jnp.concatenate([2.0 * scaled[:, None, :] * xf, (-scaled * ctf)[:, None, :]], axis=1)
        left = left.astype(jnp.bfloat16).reshape(IMG_DEV, 3 * K)
        scores = lax.dot_general(left, right, (((1,), (1,)), ((), ())), preferred_element_type=jnp.float32)
        weights = weights_of(scores, sig_rows)
        mixed = jnp.dot(weights, right, preferred_element_type=jnp.float32).reshape(IMG_DEV, 3, K)
        wsum = jnp.sum(weights.astype(jnp.float32), axis=1)
        noise = wsum[:, None] * (xf[:, 0] * xf[:, 0] + xf[:, 1] * xf[:, 1])
        noise = noise - 2.0 * ctf * (xf[:, 0] * mixed[:, 0] + xf[:, 1] * mixed[:, 1]) + ctf * ctf * mixed[:, 2]
        corrected = (ctf[:, None, :] * xf).astype(jnp.bfloat16).reshape(IMG_DEV, 2 * K)
        part = lax.dot_general(weights, corrected, (((0,), (0,)), ((), ())), preferred_element_type=jnp.float32)
        return (acc_slices + part, acc_noise + jnp.sum(noise, axis=0)), None

    init = (jnp.zeros((ORIENT, 2 * K), jnp.float32), jnp.zeros((K,), jnp.float32))
    (slices, noise), _ = lax.scan(step, init, (img_blocks, grp_blocks, sig_blocks))
    return slices.reshape(ORIENT, 2, K), noise / IMAGES
```

```python
import jax
import jax.numpy as jnp
from jax import lax
from jax.experimental import pallas as pl
from jax.experimental.pallas import tpu as pltpu
from jax.sharding import PartitionSpec as P

NX, NZ, NY = 4, 4, 8
TOP = 13.0
F32 = jnp.float32
BF16 = jnp.bfloat16
F16 = jnp.float16
PARAMS = pltpu.CompilerParams(vmem_limit_bytes=40 * 1024 * 1024)


def thirds(v):
    hi = v.astype(BF16)
    rest = v - hi.astype(F32)
    mid = rest.astype(BF16)
    low = (rest - mid.astype(F32)).astype(BF16)
    return jnp.concatenate([hi, mid, low], axis=0)


def matmul(a, b, dims):
    return lax.dot_general(a, b, (dims, ((), ())), preferred_element_type=F32)


def exponent(v):
    top = jnp.maximum(jnp.max(jnp.max(jnp.abs(v), axis=0, keepdims=True), axis=1, keepdims=True), 1e-30)
    return jnp.floor(jnp.log(top) * 1.4426950408889634)


def pre_kernel(xi, pi, table, grp, noise, sig_t, compact, corr_out, q2_out, prj_out, left, ctf, corr, q2, prj, sems):
    groups, k_dev = table.shape
    n_img = ctf.shape[0]
    orient = prj.shape[0]
    n_sig = sig_t.shape[0]
    onehot = (grp[...] == lax.broadcasted_iota(jnp.int32, (groups, n_img), 0)).astype(F32).astype(BF16)
    ctf[...] = matmul(jnp.concatenate([onehot] * 3, axis=0), thirds(table[...]), ((0,), (0,)))
    for row in range(0, n_img, 32):
        rows = slice(row, row + 32)
        x0 = xi[0, rows].astype(F32)
        x1 = xi[1, rows].astype(F32)
        c = ctf[rows]
        scaled = c * noise[...]
        twice = 2.0 * scaled
        left[rows, :k_dev] = (twice * x0).astype(BF16)
        left[rows, k_dev : 2 * k_dev] = (twice * x1).astype(BF16)
        left[rows, 2 * k_dev :] = (-scaled * c).astype(BF16)
        corr[rows, :k_dev] = (c * x0).astype(BF16)
        corr[rows, k_dev:] = (c * x1).astype(BF16)
        q2[rows] = x0 * x0 + x1 * x1
    for row in range(0, orient, 32):
        rows = slice(row, row + 32)
        prj[rows, :k_dev] = pi[0, rows]
        prj[rows, k_dev : 2 * k_dev] = pi[1, rows]
        p0 = pi[0, rows].astype(F32)
        p1 = pi[1, rows].astype(F32)
        prj[rows, 2 * k_dev :] = (p0 * p0 + p1 * p1).astype(BF16)
    copies = [
        pltpu.make_async_copy(src, dst, sems.at[n])
        for n, (src, dst) in enumerate(((corr, corr_out), (q2, q2_out), (prj, prj_out)))
    ]
    for copy in copies:
        copy.start()
    part = matmul(left[...], prj[...], ((1,), (1,)))
    sig_pad = jnp.concatenate([sig_t[...], jnp.zeros((128 - n_sig, n_img), jnp.int32)], axis=0)
    index = sig_pad.T
    first = jnp.take_along_axis(part[:, :128], jnp.minimum(index, 127), axis=1)
    rest = jnp.concatenate([part[:, 128:], jnp.zeros((n_img, 256 - orient), F32)], axis=1)
    second = jnp.take_along_axis(rest, jnp.maximum(index - 128, 0), axis=1)
    picked = jnp.where(index < 128, first, second).T[:n_sig]
    short = n_sig // 2
    for n in range(NX):
        compact[n, :n_sig] = picked[:, :128]
        compact[n, n_sig : 2 * n_sig] = picked[:, 128:256]
        compact[n, 2 * n_sig :, :64] = picked[:short, 256:]
        compact[n, 2 * n_sig :, 64:] = picked[short:, 256:]
    for copy in copies:
        copy.wait()


def relay_kernel(stack, out):
    total = (stack[0] + stack[2]) + (stack[1] + stack[3])
    for n in range(NZ):
        out[n] = total


def mid_kernel(stack, sig_t, corr_in, q2_in, prj_in, table, grp, target, total, away, mine, corr, q2, prj, sems):
    copies = [
        pltpu.make_async_copy(src, dst, sems.at[n])
        for n, (src, dst) in enumerate(((corr_in, corr), (q2_in, q2), (prj_in, prj)))
    ]
    for copy in copies:
        copy.start()
    groups, k_dev = table.shape
    n_sig, n_img = sig_t.shape
    orient = prj.shape[0]
    half = orient // 2
    packed = (stack[0] + stack[2]) + (stack[1] + stack[3])
    last = packed[2 * n_sig :]
    scores = jnp.concatenate(
        [packed[:n_sig], packed[n_sig : 2 * n_sig], jnp.concatenate([last[:, :64], last[:, 64:]], axis=0)], axis=1
    )
    expo = jnp.exp(scores - jnp.max(scores, axis=0, keepdims=True))
    w_c = (expo / jnp.sum(expo, axis=0, keepdims=True)).astype(BF16).astype(F32)
    sig = sig_t[...]
    blocks = []
    for base in range(0, orient, 64):
        ids = lax.broadcasted_iota(jnp.int32, (64, n_img), 0) + base
        acc = jnp.zeros((64, n_img), F32)
        for s in range(n_sig):
            acc = jnp.where(sig[s : s + 1] == ids, w_c[s : s + 1], acc)
        blocks.append(acc.astype(BF16))
    w_t = jnp.concatenate(blocks, axis=0)
    shuffle = (target[...] == lax.broadcasted_iota(jnp.int32, (orient, orient), 1)).astype(F32).astype(BF16)
    w_s = matmul(shuffle, w_t, ((1,), (0,))).astype(BF16)
    w_sum = matmul(w_t, jnp.ones((orient, 128), BF16), ((0,), (0,)))
    onehot = (grp[...] == lax.broadcasted_iota(jnp.int32, (groups, n_img), 0)).astype(F32).astype(BF16)
    w_g = matmul(onehot, w_t, ((1,), (1,)))
    for copy in copies:
        copy.wait()
    away[:half] = matmul(w_s[:half], corr[...], ((1,), (0,)))
    mine[:half] = matmul(w_s[half:], corr[...], ((1,), (0,)))
    mix = matmul(thirds(w_g), prj[:, 2 * k_dev :], ((1,), (0,)))
    mix = (mix[:groups] + mix[groups : 2 * groups]) + mix[2 * groups :]
    noise = jnp.sum(table[...] * table[...] * mix, axis=0, keepdims=True)
    plain = [
        jnp.sum(q2[:, at : at + 128] * w_sum, axis=0, keepdims=True) for at in range(0, k_dev, 128)
    ]
    noise = noise + jnp.concatenate(plain, axis=1)
    for c in range(2):
        at = c * k_dev
        right = matmul(shuffle, prj[:, at : at + k_dev], ((1,), (0,)))
        cross = jnp.sum(right[:half] * away[:half, at : at + k_dev], axis=0, keepdims=True)
        cross = cross + jnp.sum(right[half:] * mine[:half, at : at + k_dev], axis=0, keepdims=True)
        noise = noise - 2.0 * cross
    noise = noise * (1.0 / total)
    for ref in (away, mine):
        ref[half:] = jnp.zeros((8, 2 * k_dev), F32)
        ref[half : half + 1, :k_dev] = noise


def pack_kernel(mine, got, chunks):
    half = mine.shape[0] - 8
    k_dev = mine.shape[1] // 2
    main = 3 * k_dev // 2
    bit = k_dev // 2
    own = half // (2 * NY)
    data = mine[:half] + got[:half]
    tail = mine[half : half + 1, :k_dev] + got[half : half + 1, :k_dev]
    e_half = exponent(data)
    e_tail = exponent(tail)
    data = data * jnp.exp2(TOP - e_half)
    tail = tail * jnp.exp2(TOP - e_tail)
    wide = k_dev // 5
    side = [tail[:, n * wide : (n + 1) * wide] for n in range(5)]
    side = side + [jnp.broadcast_to(v, (1, wide)) for v in (e_half, e_tail, e_tail)]
    side = jnp.concatenate(side, axis=0)
    for d in range(2 * NY):
        rows = data[own * d : own * d + own]
        chunks[d, :own, :main] = rows[:, :main]
        for n in range(own):
            chunks[d, own + n // 3 : own + n // 3 + 1, n % 3 * bit : n % 3 * bit + bit] = rows[n : n + 1, main:]
        chunks[d, :, main:] = side


def end_kernel(owned, chunks, slices, spectrum):
    k_dev = slices.shape[2]
    main = 3 * k_dev // 2
    bit = k_dev // 2
    data = jnp.zeros((8, main), F32)
    tail = jnp.zeros((8, k_dev // 5), F32)
    for d in range(2 * NY):
        side = chunks[d, :, main:]
        data = data + chunks[d, :, :main] * jnp.exp2(side[5:6, :1] - TOP)
        tail = tail + side * jnp.exp2(side[6:7, :1] - TOP)
    slices[:, 0, :] = data[:owned, :k_dev]
    slices[:, 1, :bit] = data[:owned, k_dev:]
    for n in range(owned):
        slices[n : n + 1, 1, bit:] = data[owned + n // 3 : owned + n // 3 + 1, n % 3 * bit : n % 3 * bit + bit]
    spectrum[...] = jnp.concatenate([tail[n : n + 1] for n in range(5)], axis=1)


VM = pl.BlockSpec(memory_space=pltpu.VMEM)
HB = pl.BlockSpec(memory_space=pltpu.HBM)


def call(body, ins, outs, scratch=()):
    shapes = [jax.ShapeDtypeStruct(s, t) for s, t, _ in outs]
    return pl.pallas_call(
        body,
        in_specs=ins,
        out_specs=[where for _, _, where in outs],
        out_shape=shapes,
        scratch_shapes=list(scratch),
        compiler_params=PARAMS,
    )


def spread(v, axis, groups=None):
    return lax.all_to_all(v, axis, 0, 0, axis_index_groups=groups, tiled=True)


def img_shift(v, dh, dc):
    perm = []
    for h in range(2):
        for y in range(NY):
            for c in range(2):
                perm.append(((h * NY + y) * 2 + c, ((h + dh) % 2 * NY + y) * 2 + (c + dc) % 2))
    return lax.ppermute(v, "img", perm)


def pre(images, projections, ctf_table, grp, noise_weight, sig_t):
    n_img, _, k_dev = images.shape
    orient = projections.shape[0]
    carried = [((n_img, 2 * k_dev), BF16), ((n_img, k_dev), F32), ((orient, 3 * k_dev), BF16)]
    packed = (NX, sig_t.shape[0] * n_img // 128, 128)
    return call(
        pre_kernel,
        [VM] * 6,
        [(packed, F32, VM)] + [(s, t, HB) for s, t in carried],
        [pltpu.VMEM((n_img, 3 * k_dev), BF16), pltpu.VMEM((n_img, k_dev), F32)]
        + [pltpu.VMEM(s, t) for s, t in carried]
        + [pltpu.SemaphoreType.DMA((3,))],
    )(
        images.transpose(1, 0, 2),
        projections.transpose(1, 0, 2),
        ctf_table,
        grp,
        noise_weight[None],
        sig_t,
    )


def mid(stack, sig_t, corr, q2, prj, ctf_table, grp, target, total):
    orient, k_dev = prj.shape[0], ctf_table.shape[1]

    def body(*refs):
        mid_kernel(*refs[:8], total, *refs[8:])

    shape = ((orient // 2 + 8, 2 * k_dev), F32, VM)
    return call(
        body,
        [VM, VM, HB, HB, HB, VM, VM, VM],
        [shape, shape],
        [pltpu.VMEM(v.shape, v.dtype) for v in (corr, q2, prj)] + [pltpu.SemaphoreType.DMA((3,))],
    )(stack, sig_t, corr, q2, prj, ctf_table, grp, target)


def targets(me, orient, owned):
    pos = jnp.arange(orient, dtype=jnp.int32)
    a, h = pos // (orient // 2), pos % (orient // 2)
    owner = h // owned * 2 + (me + 1 - a) % 2
    return (owner * owned + h % owned)[:, None]


def per_device(images, projections, ctf_table, ctf_group, noise_weight, significant):
    img_rows, _, k_dev = images.shape
    orient = projections.shape[0]
    owned = orient // lax.axis_size("img")
    total = img_rows * lax.axis_size("img")
    grp = ctf_group[None]
    sig_t = significant.T
    compact, corr, q2, prj = pre(images, projections, ctf_table, grp, noise_weight, sig_t)
    along_x = [[z * NX + x for x in range(NX)] for z in range(NZ)]
    along_z = [[z * NX + x for z in range(NZ)] for x in range(NX)]
    compact = spread(compact, "blk", along_x)
    compact = call(relay_kernel, [VM], [(compact.shape, F32, VM)])(compact)[0]
    stack = spread(compact, "blk", along_z)
    target = targets(lax.axis_index("img"), orient, owned)
    away, mine = mid(stack, sig_t, corr, q2, prj, ctf_table, grp, target, total)
    got = img_shift(away, 0, 1)
    shape = (2 * NY, 8, 3 * k_dev // 2 + k_dev // 5)
    chunks = call(pack_kernel, [VM, VM], [(shape, F32, VM)])(mine, got)[0].astype(F16)
    peers = [[n * 2 + c for n in range(2 * NY)] for c in range(2)]
    chunks = spread(chunks, "img", peers).astype(F32)

    def body(*refs):
        end_kernel(owned, *refs)

    slices, spectrum = call(body, [VM], [((owned, 2, k_dev), F32, VM), ((1, k_dev), F32, VM)])(chunks)
    return (slices, spectrum[0])


def solution(mesh):
    return jax.shard_map(
        per_device,
        mesh=mesh,
        in_specs=(
            P("img", None, "blk"),
            P(None, None, "blk"),
            P(None, "blk"),
            P("img"),
            P("blk"),
            P("img", None),
        ),
        out_specs=(P("img", None, "blk"), P("blk")),
        check_vma=False,
    )
```

```python
import jax
import jax.numpy as jnp
from jax import lax
from jax.experimental import pallas as pl
from jax.experimental.pallas import tpu as pltpu
from jax.sharding import PartitionSpec as P

NX, NZ, NY = 4, 4, 8
TOP = 13.0
F32 = jnp.float32
BF16 = jnp.bfloat16
F16 = jnp.float16
PARAMS = pltpu.CompilerParams(vmem_limit_bytes=24 * 1024 * 1024)


def thirds(v):
    hi = v.astype(BF16)
    rest = v - hi.astype(F32)
    mid = rest.astype(BF16)
    low = (rest - mid.astype(F32)).astype(BF16)
    return jnp.concatenate([hi, mid, low], axis=0)


def matmul(a, b, dims):
    return lax.dot_general(a, b, (dims, ((), ())), preferred_element_type=F32)


def exponent(v):
    top = jnp.maximum(jnp.max(jnp.max(jnp.abs(v), axis=0, keepdims=True), axis=1, keepdims=True), 1e-30)
    return jnp.floor(jnp.log(top) * 1.4426950408889634)


def pre_kernel(xi, pi, table, grp, noise, sig_t, compact, corr, q2, prj, left, ctf):
    groups, k_dev = table.shape
    n_img = ctf.shape[0]
    orient = prj.shape[0]
    n_sig = sig_t.shape[0]
    onehot = (grp[...][None, :] == lax.broadcasted_iota(jnp.int32, (groups, n_img), 0)).astype(F32).astype(BF16)
    weight = noise[...][None, :]
    ctf[...] = matmul(jnp.concatenate([onehot] * 3, axis=0), thirds(table[...]), ((0,), (0,)))
    for row in range(0, n_img, 32):
        rows = slice(row, row + 32)
        x0 = xi[0, rows].astype(F32)
        x1 = xi[1, rows].astype(F32)
        c = ctf[rows]
        scaled = c * weight
        twice = 2.0 * scaled
        left[rows, :k_dev] = (twice * x0).astype(BF16)
        left[rows, k_dev : 2 * k_dev] = (twice * x1).astype(BF16)
        left[rows, 2 * k_dev :] = (-scaled * c).astype(BF16)
        corr[rows, :k_dev] = (c * x0).astype(BF16)
        corr[rows, k_dev:] = (c * x1).astype(BF16)
        q2[rows] = x0 * x0 + x1 * x1
    for row in range(0, orient, 32):
        rows = slice(row, row + 32)
        prj[rows, :k_dev] = pi[0, rows]
        prj[rows, k_dev : 2 * k_dev] = pi[1, rows]
        p0 = pi[0, rows].astype(F32)
        p1 = pi[1, rows].astype(F32)
        prj[rows, 2 * k_dev :] = (p0 * p0 + p1 * p1).astype(BF16)
    part = matmul(left[...], prj[...], ((1,), (1,)))
    sig_pad = jnp.concatenate([sig_t[...], jnp.zeros((128 - n_sig, n_img), jnp.int32)], axis=0)
    index = sig_pad.T
    first = jnp.take_along_axis(part[:, :128], jnp.minimum(index, 127), axis=1)
    rest = jnp.concatenate([part[:, 128:], jnp.zeros((n_img, 256 - orient), F32)], axis=1)
    second = jnp.take_along_axis(rest, jnp.maximum(index - 128, 0), axis=1)
    picked = jnp.where(index < 128, first, second).T[:n_sig]
    short = n_sig // 2
    for n in range(NX):
        compact[n, :n_sig] = picked[:, :128]
        compact[n, n_sig : 2 * n_sig] = picked[:, 128:256]
        compact[n, 2 * n_sig :, :64] = picked[:short, 256:]
        compact[n, 2 * n_sig :, 64:] = picked[short:, 256:]


def relay_kernel(stack, out):
    total = (stack[0] + stack[2]) + (stack[1] + stack[3])
    for n in range(NZ):
        out[n] = total


def targets(me, orient, owned):
    my_h, my_c = me // (2 * NY), me % 2
    pos = lax.broadcasted_iota(jnp.int32, (orient, orient), 0)
    a = jnp.where(pos < orient // 2, 0, 1)
    h = pos - a * (orient // 2)
    d = jnp.where(h < 8 * NY, h >> 3, (h - 8 * NY) >> 2)
    q = jnp.where(h < 8 * NY, h & 7, 8 + (h & 3))
    b = jnp.where(q < owned, 0, 1)
    owner = (((my_h + 1 - b) & 1) * NY + d) * 2 + ((my_c + 1 - a) & 1)
    return owner * owned + q - b * owned


def mid_kernel(stack, sig_t, corr, q2, prj, table, grp, total, away, mine):
    groups, k_dev = table.shape
    n_sig, n_img = sig_t.shape
    orient = prj.shape[0]
    half = orient // 2
    packed = (stack[0] + stack[2]) + (stack[1] + stack[3])
    last = packed[2 * n_sig :]
    scores = jnp.concatenate(
        [packed[:n_sig], packed[n_sig : 2 * n_sig], jnp.concatenate([last[:, :64], last[:, 64:]], axis=0)], axis=1
    )
    expo = jnp.exp(scores - jnp.max(scores, axis=0, keepdims=True))
    w_c = (expo / jnp.sum(expo, axis=0, keepdims=True)).astype(BF16).astype(F32)
    sig = sig_t[...]
    blocks = []
    for base in range(0, orient, 64):
        ids = lax.broadcasted_iota(jnp.int32, (64, n_img), 0) + base
        acc = jnp.zeros((64, n_img), F32)
        for s in range(n_sig):
            acc = jnp.where(sig[s : s + 1] == ids, w_c[s : s + 1], acc)
        blocks.append(acc.astype(BF16))
    w_t = jnp.concatenate(blocks, axis=0)
    target = targets(lax.axis_index("img"), orient, orient // (4 * NY))
    shuffle = (target == lax.broadcasted_iota(jnp.int32, (orient, orient), 1)).astype(F32).astype(BF16)
    w_s = matmul(shuffle, w_t, ((1,), (0,))).astype(BF16)
    w_sum = matmul(w_t, jnp.ones((orient, 128), BF16), ((0,), (0,)))
    onehot = (grp[...][None, :] == lax.broadcasted_iota(jnp.int32, (groups, n_img), 0)).astype(F32).astype(BF16)
    w_g = matmul(onehot, w_t, ((1,), (1,)))
    away[:half] = matmul(w_s[:half], corr[...], ((1,), (0,)))
    mine[:half] = matmul(w_s[half:], corr[...], ((1,), (0,)))
    mix = matmul(thirds(w_g), prj[:, 2 * k_dev :], ((1,), (0,)))
    mix = (mix[:groups] + mix[groups : 2 * groups]) + mix[2 * groups :]
    noise = jnp.sum(table[...] * table[...] * mix, axis=0, keepdims=True)
    plain = [
        jnp.sum(q2[:, at : at + 128] * w_sum, axis=0, keepdims=True) for at in range(0, k_dev, 128)
    ]
    noise = noise + jnp.concatenate(plain, axis=1)
    for c in range(2):
        at = c * k_dev
        right = matmul(shuffle, prj[:, at : at + k_dev], ((1,), (0,)))
        cross = jnp.sum(right[:half] * away[:half, at : at + k_dev], axis=0, keepdims=True)
        cross = cross + jnp.sum(right[half:] * mine[:half, at : at + k_dev], axis=0, keepdims=True)
        noise = noise - 2.0 * cross
    noise = noise * (1.0 / total)
    for ref in (away, mine):
        ref[half:] = jnp.zeros((8, 2 * k_dev), F32)
        ref[half : half + 1, :k_dev] = noise


def pack_kernel(mine, got, chunks):
    half = mine.shape[0] - 8
    k_dev = mine.shape[1] // 2
    data = mine[:half] + got[:half]
    tail = mine[half : half + 1, :k_dev] + got[half : half + 1, :k_dev]
    e_half = exponent(data)
    e_tail = exponent(tail)
    data = data * jnp.exp2(TOP - e_half)
    tail = tail * jnp.exp2(TOP - e_tail)
    wide = k_dev // 5
    side = [tail[:, n * wide : (n + 1) * wide] for n in range(5)]
    side = side + [jnp.broadcast_to(v, (1, wide)) for v in (e_half, e_tail, e_tail)]
    side = jnp.concatenate(side, axis=0)
    for d in range(NY):
        chunks[d, :, : 2 * k_dev] = data[8 * d : 8 * d + 8]
        low = data[8 * NY + 4 * d : 8 * NY + 4 * d + 4]
        chunks[d, :4, 2 * k_dev : 3 * k_dev] = low[:, :k_dev]
        chunks[d, 4:, 2 * k_dev : 3 * k_dev] = low[:, k_dev:]
        chunks[d, :, 3 * k_dev :] = side


def sum_kernel(owned, chunks, send, keep, last):
    k_dev = last.shape[1]
    data = jnp.zeros((8, 3 * k_dev), F32)
    tail = jnp.zeros((8, k_dev // 5), F32)
    e_half = None
    for d in range(NY):
        side = chunks[d, :, 3 * k_dev :]
        one, two = side[5:6, :1], side[6:7, :1]
        data = data + chunks[d, :, : 3 * k_dev] * jnp.exp2(one - TOP)
        tail = tail + side * jnp.exp2(two - TOP)
        e_half = one if d == 0 else jnp.maximum(e_half, one)
        e_tail = two if d == 0 else jnp.maximum(e_tail, two)
    row = jnp.concatenate([tail[n : n + 1] for n in range(5)], axis=1)
    send[:owned] = data[:owned, : 2 * k_dev] * jnp.exp2(TOP - 3.0 - e_half)
    send[owned : owned + 1, :k_dev] = row * jnp.exp2(TOP - 3.0 - e_tail)
    send[owned : owned + 1, k_dev : k_dev + 128] = jnp.broadcast_to(e_half, (1, 128))
    send[owned : owned + 1, k_dev + 128 :] = jnp.broadcast_to(e_tail, (1, k_dev - 128))
    send[owned + 1 :] = jnp.zeros((7 - owned, 2 * k_dev), F32)
    left = 8 - owned
    for c in range(2):
        at = c * k_dev
        keep[:left, at : at + k_dev] = data[owned:, at : at + k_dev]
        keep[left:owned, at : at + k_dev] = data[4 * c : 4 * c + 4, 2 * k_dev : 3 * k_dev]
    keep[owned:] = jnp.zeros((8 - owned, 2 * k_dev), F32)
    last[...] = row


def end_kernel(owned, keep, last, got, slices, spectrum):
    k_dev = last.shape[1]
    grow = jnp.exp2(got[owned : owned + 1, k_dev : k_dev + 1] - (TOP - 3.0))
    grow_tail = jnp.exp2(got[owned : owned + 1, k_dev + 128 : k_dev + 129] - (TOP - 3.0))
    out = keep[:owned] + got[:owned] * grow
    for c in range(2):
        slices[:, c, :] = out[:, c * k_dev : (c + 1) * k_dev]
    spectrum[...] = (last[...] + got[owned : owned + 1, :k_dev] * grow_tail).reshape(k_dev)


VM = pl.BlockSpec(memory_space=pltpu.VMEM)


def call(body, ins, outs, scratch=()):
    return pl.pallas_call(
        body,
        in_specs=[VM] * ins,
        out_specs=[VM] * len(outs),
        out_shape=[jax.ShapeDtypeStruct(s, t) for s, t in outs],
        scratch_shapes=list(scratch),
        compiler_params=PARAMS,
    )


def spread(v, axis, groups=None):
    return lax.all_to_all(v, axis, 0, 0, axis_index_groups=groups, tiled=True)


def img_shift(v, dh, dc):
    perm = []
    for h in range(2):
        for y in range(NY):
            for c in range(2):
                to = (h + dh) % 2 * NY + y
                perm.append(((h * NY + y) * 2 + c, to * 2 + (c + dc) % 2))
    return lax.ppermute(v, "img", perm)


def pre(images, projections, ctf_table, grp, noise_weight, sig_t):
    n_img, _, k_dev = images.shape
    orient = projections.shape[0]
    packed = (NX, sig_t.shape[0] * n_img // 128, 128)
    return call(
        pre_kernel,
        6,
        [
            (packed, F32),
            ((n_img, 2 * k_dev), BF16),
            ((n_img, k_dev), F32),
            ((orient, 3 * k_dev), BF16),
        ],
        [pltpu.VMEM((n_img, 3 * k_dev), BF16), pltpu.VMEM((n_img, k_dev), F32)],
    )(
        images.transpose(1, 0, 2),
        projections.transpose(1, 0, 2),
        ctf_table,
        grp,
        noise_weight,
        sig_t,
    )


def mid(stack, sig_t, corr, q2, prj, ctf_table, grp, total):
    orient, k_dev = prj.shape[0], ctf_table.shape[1]

    def body(*refs):
        mid_kernel(*refs[:7], total, *refs[7:])

    shape = ((orient // 2 + 8, 2 * k_dev), F32)
    return call(body, 7, [shape, shape])(stack, sig_t, corr, q2, prj, ctf_table, grp)


def per_device(images, projections, ctf_table, ctf_group, noise_weight, significant):
    img_rows, _, k_dev = images.shape
    orient = projections.shape[0]
    owned = orient // lax.axis_size("img")
    total = img_rows * lax.axis_size("img")
    sig_t = significant.T
    compact, corr, q2, prj = pre(images, projections, ctf_table, ctf_group, noise_weight, sig_t)
    along_x = [[z * NX + x for x in range(NX)] for z in range(NZ)]
    along_z = [[z * NX + x for z in range(NZ)] for x in range(NX)]
    compact = spread(compact, "blk", along_x)
    compact = call(relay_kernel, 1, [(compact.shape, F32)])(compact)[0]
    stack = spread(compact, "blk", along_z)
    away, mine = mid(stack, sig_t, corr, q2, prj, ctf_table, ctf_group, total)
    got = img_shift(away, 0, 1)
    shape = (8, 3 * k_dev + k_dev // 5)
    chunks = call(pack_kernel, 2, [((NY,) + shape, F32)])(mine, got)[0]
    along_y = [[(h * NY + y) * 2 + c for y in range(NY)] for h in range(2) for c in range(2)]
    chunks = spread(chunks.astype(F16), "img", along_y).astype(F32)
    wide = (8, 2 * k_dev)

    def add(*refs):
        sum_kernel(owned, *refs)

    def end(*refs):
        end_kernel(owned, *refs)

    send, keep, last = call(add, 1, [(wide, F32), (wide, F32), ((1, k_dev), F32)])(chunks)
    got = img_shift(send.astype(F16), 1, 0).astype(F32)
    slices, spectrum = call(end, 3, [((owned, 2, k_dev), F32), ((k_dev,), F32)])(keep, last, got)
    return (slices, spectrum)


def solution(mesh):
    return jax.shard_map(
        per_device,
        mesh=mesh,
        in_specs=(
            P("img", None, "blk"),
            P(None, None, "blk"),
            P(None, "blk"),
            P("img"),
            P("blk"),
            P("img", None),
        ),
        out_specs=(P("img", None, "blk"), P("blk")),
        check_vma=False,
    )
```

```python
import jax
import jax.numpy as jnp
from jax import lax
from jax.experimental import pallas as pl
from jax.experimental.pallas import tpu as pltpu
from jax.sharding import PartitionSpec as P

NX, NZ, NY = 4, 4, 8
TOP = 13.0
ORDER = (0, 4, 2, 6, 1, 5, 3, 7)
FOUR = (0, 2, 1, 3)
F32 = jnp.float32
BF16 = jnp.bfloat16
F16 = jnp.float16
PARAMS = pltpu.CompilerParams(vmem_limit_bytes=24 * 1024 * 1024)


def thirds(v):
    hi = v.astype(BF16)
    rest = v - hi.astype(F32)
    mid = rest.astype(BF16)
    low = (rest - mid.astype(F32)).astype(BF16)
    return jnp.concatenate([hi, mid, low], axis=0)


def matmul(a, b, dims):
    return lax.dot_general(a, b, (dims, ((), ())), preferred_element_type=F32)


def exponent(v):
    top = jnp.maximum(jnp.max(jnp.max(jnp.abs(v), axis=0, keepdims=True), axis=1, keepdims=True), 1e-30)
    return jnp.floor(jnp.log(top) * 1.4426950408889634)


def pre_kernel(xi, pi, table, grp, noise, sig_t, compact, corr, q2, prj, left, ctf):
    groups, k_dev = table.shape
    n_img = ctf.shape[0]
    orient = prj.shape[0]
    n_sig = sig_t.shape[0]
    onehot = (grp[...][None, :] == lax.broadcasted_iota(jnp.int32, (groups, n_img), 0)).astype(F32).astype(BF16)
    weight = noise[...][None, :]
    ctf[...] = matmul(jnp.concatenate([onehot] * 3, axis=0), thirds(table[...]), ((0,), (0,)))
    for row in range(0, n_img, 32):
        rows = slice(row, row + 32)
        x0 = xi[0, rows].astype(F32)
        x1 = xi[1, rows].astype(F32)
        c = ctf[rows]
        scaled = c * weight
        twice = 2.0 * scaled
        left[rows, :k_dev] = (twice * x0).astype(BF16)
        left[rows, k_dev : 2 * k_dev] = (twice * x1).astype(BF16)
        left[rows, 2 * k_dev :] = (-scaled * c).astype(BF16)
        corr[rows, :k_dev] = (c * x0).astype(BF16)
        corr[rows, k_dev:] = (c * x1).astype(BF16)
        q2[rows] = x0 * x0 + x1 * x1
    for row in range(0, orient, 32):
        rows = slice(row, row + 32)
        prj[rows, :k_dev] = pi[0, rows]
        prj[rows, k_dev : 2 * k_dev] = pi[1, rows]
        p0 = pi[0, rows].astype(F32)
        p1 = pi[1, rows].astype(F32)
        prj[rows, 2 * k_dev :] = (p0 * p0 + p1 * p1).astype(BF16)
    part = matmul(left[...], prj[...], ((1,), (1,)))
    sig_pad = jnp.concatenate([sig_t[...], jnp.zeros((128 - n_sig, n_img), jnp.int32)], axis=0)
    index = sig_pad.T
    first = jnp.take_along_axis(part[:, :128], jnp.minimum(index, 127), axis=1)
    rest = jnp.concatenate([part[:, 128:], jnp.zeros((n_img, 256 - orient), F32)], axis=1)
    second = jnp.take_along_axis(rest, jnp.maximum(index - 128, 0), axis=1)
    picked = jnp.where(index < 128, first, second).T[:n_sig]
    short = n_sig // 2
    for n in range(NX):
        compact[n, :n_sig] = picked[:, :128]
        compact[n, n_sig : 2 * n_sig] = picked[:, 128:256]
        compact[n, 2 * n_sig :, :64] = picked[:short, 256:]
        compact[n, 2 * n_sig :, 64:] = picked[short:, 256:]


def relay_kernel(stack, out):
    total = (stack[0] + stack[2]) + (stack[1] + stack[3])
    for n in range(NZ):
        out[n] = total


def targets(me, orient, owned):
    my_h, my_c = me // (2 * NY), me % 2
    pos = lax.broadcasted_iota(jnp.int32, (orient, orient), 0)
    a = jnp.where(pos < orient // 2, 0, 1)
    h = pos - a * (orient // 2)
    d = jnp.where(h < 8 * NY, h >> 3, (h - 8 * NY) >> 2)
    q = jnp.where(h < 8 * NY, h & 7, 8 + (h & 3))
    b = jnp.where(q < owned, 0, 1)
    y = ((d & 1) << 2) + (d & 2) + (d >> 2)
    owner = (((my_h + 1 - b) & 1) * NY + y) * 2 + ((my_c + 1 - a) & 1)
    return owner * owned + q - b * owned


def mid_kernel(stack, sig_t, corr, q2, prj, table, grp, total, away, mine):
    groups, k_dev = table.shape
    n_sig, n_img = sig_t.shape
    orient = prj.shape[0]
    half = orient // 2
    packed = (stack[0] + stack[2]) + (stack[1] + stack[3])
    last = packed[2 * n_sig :]
    scores = jnp.concatenate(
        [packed[:n_sig], packed[n_sig : 2 * n_sig], jnp.concatenate([last[:, :64], last[:, 64:]], axis=0)], axis=1
    )
    expo = jnp.exp(scores - jnp.max(scores, axis=0, keepdims=True))
    w_c = (expo / jnp.sum(expo, axis=0, keepdims=True)).astype(BF16).astype(F32)
    sig = sig_t[...]
    blocks = []
    for base in range(0, orient, 64):
        ids = lax.broadcasted_iota(jnp.int32, (64, n_img), 0) + base
        acc = jnp.zeros((64, n_img), F32)
        for s in range(n_sig):
            acc = jnp.where(sig[s : s + 1] == ids, w_c[s : s + 1], acc)
        blocks.append(acc.astype(BF16))
    w_t = jnp.concatenate(blocks, axis=0)
    target = targets(lax.axis_index("img"), orient, orient // (4 * NY))
    shuffle = (target == lax.broadcasted_iota(jnp.int32, (orient, orient), 1)).astype(F32).astype(BF16)
    w_s = matmul(shuffle, w_t, ((1,), (0,))).astype(BF16)
    w_sum = matmul(w_t, jnp.ones((orient, 128), BF16), ((0,), (0,)))
    onehot = (grp[...][None, :] == lax.broadcasted_iota(jnp.int32, (groups, n_img), 0)).astype(F32).astype(BF16)
    w_g = matmul(onehot, w_t, ((1,), (1,)))
    away[:half] = matmul(w_s[:half], corr[...], ((1,), (0,)))
    mine[:half] = matmul(w_s[half:], corr[...], ((1,), (0,)))
    mix = matmul(thirds(w_g), prj[:, 2 * k_dev :], ((1,), (0,)))
    mix = (mix[:groups] + mix[groups : 2 * groups]) + mix[2 * groups :]
    noise = jnp.sum(table[...] * table[...] * mix, axis=0, keepdims=True)
    plain = [
        jnp.sum(q2[:, at : at + 128] * w_sum, axis=0, keepdims=True) for at in range(0, k_dev, 128)
    ]
    noise = noise + jnp.concatenate(plain, axis=1)
    for c in range(2):
        at = c * k_dev
        right = matmul(shuffle, prj[:, at : at + k_dev], ((1,), (0,)))
        cross = jnp.sum(right[:half] * away[:half, at : at + k_dev], axis=0, keepdims=True)
        cross = cross + jnp.sum(right[half:] * mine[:half, at : at + k_dev], axis=0, keepdims=True)
        noise = noise - 2.0 * cross
    noise = noise * (1.0 / total)
    e_half = exponent(away[:half])
    e_tail = exponent(noise)
    away[:half] = away[:half] * jnp.exp2(TOP - e_half)
    away[half:] = jnp.zeros((8, 2 * k_dev), F32)
    away[half : half + 1, :k_dev] = noise * jnp.exp2(TOP - e_tail)
    away[half : half + 1, k_dev : k_dev + 128] = jnp.broadcast_to(e_half, (1, 128))
    away[half : half + 1, k_dev + 128 :] = jnp.broadcast_to(e_tail, (1, k_dev - 128))
    mine[half:] = jnp.zeros((8, 2 * k_dev), F32)
    mine[half : half + 1, :k_dev] = noise


def pack_kernel(mine, got, chunks):
    half = mine.shape[0] - 8
    k_dev = mine.shape[1] // 2
    e_half = got[half : half + 1, k_dev : k_dev + 1]
    e_tail = got[half : half + 1, k_dev + 128 : k_dev + 129]
    data = mine[:half] + got[:half] * jnp.exp2(e_half - TOP)
    tail = mine[half : half + 1, :k_dev] + got[half : half + 1, :k_dev] * jnp.exp2(e_tail - TOP)
    e_half = exponent(data)
    e_tail = exponent(tail)
    data = data * jnp.exp2(TOP - e_half)
    tail = tail * jnp.exp2(TOP - e_tail)
    wide = k_dev // 5
    side = [tail[:, n * wide : (n + 1) * wide] for n in range(5)]
    side = side + [jnp.broadcast_to(v, (1, wide)) for v in (e_half, e_tail, e_tail)]
    side = jnp.concatenate(side, axis=0)
    for d in range(NY):
        chunks[d, :, : 2 * k_dev] = data[8 * d : 8 * d + 8]
        low = data[8 * NY + 4 * d : 8 * NY + 4 * d + 4]
        chunks[d, :4, 2 * k_dev : 3 * k_dev] = low[:, :k_dev]
        chunks[d, 4:, 2 * k_dev : 3 * k_dev] = low[:, k_dev:]
        chunks[d, :, 3 * k_dev :] = side


def sum_kernel(owned, chunks, send, keep, last):
    k_dev = last.shape[1]
    data = jnp.zeros((8, 3 * k_dev), F32)
    tail = jnp.zeros((8, k_dev // 5), F32)
    e_half = None
    for d in range(NY):
        side = chunks[d, :, 3 * k_dev :]
        one, two = side[5:6, :1], side[6:7, :1]
        data = data + chunks[d, :, : 3 * k_dev] * jnp.exp2(one - TOP)
        tail = tail + side * jnp.exp2(two - TOP)
        e_half = one if d == 0 else jnp.maximum(e_half, one)
        e_tail = two if d == 0 else jnp.maximum(e_tail, two)
    row = jnp.concatenate([tail[n : n + 1] for n in range(5)], axis=1)
    send[:owned] = data[:owned, : 2 * k_dev] * jnp.exp2(TOP - 3.0 - e_half)
    send[owned : owned + 1, :k_dev] = row * jnp.exp2(TOP - 3.0 - e_tail)
    send[owned : owned + 1, k_dev : k_dev + 128] = jnp.broadcast_to(e_half, (1, 128))
    send[owned : owned + 1, k_dev + 128 :] = jnp.broadcast_to(e_tail, (1, k_dev - 128))
    send[owned + 1 :] = jnp.zeros((7 - owned, 2 * k_dev), F32)
    left = 8 - owned
    for c in range(2):
        at = c * k_dev
        keep[:left, at : at + k_dev] = data[owned:, at : at + k_dev]
        keep[left:owned, at : at + k_dev] = data[4 * c : 4 * c + 4, 2 * k_dev : 3 * k_dev]
    keep[owned:] = jnp.zeros((8 - owned, 2 * k_dev), F32)
    last[...] = row


def end_kernel(owned, keep, last, got, slices, spectrum):
    k_dev = last.shape[1]
    grow = jnp.exp2(got[owned : owned + 1, k_dev : k_dev + 1] - (TOP - 3.0))
    grow_tail = jnp.exp2(got[owned : owned + 1, k_dev + 128 : k_dev + 129] - (TOP - 3.0))
    out = keep[:owned] + got[:owned] * grow
    for c in range(2):
        slices[:, c, :] = out[:, c * k_dev : (c + 1) * k_dev]
    spectrum[...] = (last[...] + got[owned : owned + 1, :k_dev] * grow_tail).reshape(k_dev)


VM = pl.BlockSpec(memory_space=pltpu.VMEM)


def call(body, ins, outs, scratch=()):
    return pl.pallas_call(
        body,
        in_specs=[VM] * ins,
        out_specs=[VM] * len(outs),
        out_shape=[jax.ShapeDtypeStruct(s, t) for s, t in outs],
        scratch_shapes=list(scratch),
        compiler_params=PARAMS,
    )


def spread(v, axis, groups=None):
    return lax.all_to_all(v, axis, 0, 0, axis_index_groups=groups, tiled=True)


def img_shift(v, dh, dc):
    perm = []
    for h in range(2):
        for y in range(NY):
            for c in range(2):
                to = (h + dh) % 2 * NY + y
                perm.append(((h * NY + y) * 2 + c, to * 2 + (c + dc) % 2))
    return lax.ppermute(v, "img", perm)


def pre(images, projections, ctf_table, grp, noise_weight, sig_t):
    n_img, _, k_dev = images.shape
    orient = projections.shape[0]
    packed = (NX, sig_t.shape[0] * n_img // 128, 128)
    return call(
        pre_kernel,
        6,
        [
            (packed, F32),
            ((n_img, 2 * k_dev), BF16),
            ((n_img, k_dev), F32),
            ((orient, 3 * k_dev), BF16),
        ],
        [pltpu.VMEM((n_img, 3 * k_dev), BF16), pltpu.VMEM((n_img, k_dev), F32)],
    )(
        images.transpose(1, 0, 2),
        projections.transpose(1, 0, 2),
        ctf_table,
        grp,
        noise_weight,
        sig_t,
    )


def mid(stack, sig_t, corr, q2, prj, ctf_table, grp, total):
    orient, k_dev = prj.shape[0], ctf_table.shape[1]

    def body(*refs):
        mid_kernel(*refs[:7], total, *refs[7:])

    shape = ((orient // 2 + 8, 2 * k_dev), F32)
    return call(body, 7, [shape, shape])(stack, sig_t, corr, q2, prj, ctf_table, grp)


def per_device(images, projections, ctf_table, ctf_group, noise_weight, significant):
    img_rows, _, k_dev = images.shape
    orient = projections.shape[0]
    owned = orient // lax.axis_size("img")
    total = img_rows * lax.axis_size("img")
    sig_t = significant.T
    compact, corr, q2, prj = pre(images, projections, ctf_table, ctf_group, noise_weight, sig_t)
    along_x = [[z * NX + x for x in FOUR] for z in range(NZ)]
    along_z = [[z * NX + x for z in FOUR] for x in range(NX)]
    compact = spread(compact, "blk", along_x)
    compact = call(relay_kernel, 1, [(compact.shape, F32)])(compact)[0]
    stack = spread(compact, "blk", along_z)
    away, mine = mid(stack, sig_t, corr, q2, prj, ctf_table, ctf_group, total)
    got = img_shift(away.astype(F16), 0, 1).astype(F32)
    shape = (8, 3 * k_dev + k_dev // 5)
    chunks = call(pack_kernel, 2, [((NY,) + shape, F32)])(mine, got)[0]
    along_y = [[(h * NY + y) * 2 + c for y in ORDER] for h in range(2) for c in range(2)]
    chunks = spread(chunks.astype(F16), "img", along_y).astype(F32)
    wide = (8, 2 * k_dev)

    def add(*refs):
        sum_kernel(owned, *refs)

    def end(*refs):
        end_kernel(owned, *refs)

    send, keep, last = call(add, 1, [(wide, F32), (wide, F32), ((1, k_dev), F32)])(chunks)
    got = img_shift(send.astype(F16), 1, 0).astype(F32)
    slices, spectrum = call(end, 3, [((owned, 2, k_dev), F32), ((k_dev,), F32)])(keep, last, got)
    return (slices, spectrum)


def solution(mesh):
    return jax.shard_map(
        per_device,
        mesh=mesh,
        in_specs=(
            P("img", None, "blk"),
            P(None, None, "blk"),
            P(None, "blk"),
            P("img"),
            P("blk"),
            P("img", None),
        ),
        out_specs=(P("img", None, "blk"), P("blk")),
        check_vma=False,
    )
```

```python
import jax
import jax.numpy as jnp
from jax import lax
from jax.experimental import pallas as pl
from jax.experimental.pallas import tpu as pltpu
from jax.sharding import PartitionSpec as P

NX, NZ, NY = 4, 4, 8
TOP = 13.0
ORDER = (0, 4, 1, 5, 2, 6, 3, 7)
FOUR = (0, 2, 1, 3)
F32 = jnp.float32
BF16 = jnp.bfloat16
F16 = jnp.float16
PARAMS = pltpu.CompilerParams(vmem_limit_bytes=24 * 1024 * 1024)


def thirds(v):
    hi = v.astype(BF16)
    rest = v - hi.astype(F32)
    mid = rest.astype(BF16)
    low = (rest - mid.astype(F32)).astype(BF16)
    return jnp.concatenate([hi, mid, low], axis=0)


def matmul(a, b, dims):
    return lax.dot_general(a, b, (dims, ((), ())), preferred_element_type=F32)


def exponent(v):
    top = jnp.maximum(jnp.max(jnp.max(jnp.abs(v), axis=0, keepdims=True), axis=1, keepdims=True), 1e-30)
    return jnp.floor(jnp.log(top) * 1.4426950408889634)


def pre_kernel(xi, pi, table, grp, noise, sig_t, compact, corr, q2, prj, left, ctf):
    groups, k_dev = table.shape
    n_img = ctf.shape[0]
    orient = prj.shape[0]
    n_sig = sig_t.shape[0]
    onehot = (grp[...][None, :] == lax.broadcasted_iota(jnp.int32, (groups, n_img), 0)).astype(F32).astype(BF16)
    weight = noise[...][None, :]
    ctf[...] = matmul(jnp.concatenate([onehot] * 3, axis=0), thirds(table[...]), ((0,), (0,)))
    for row in range(0, n_img, 32):
        rows = slice(row, row + 32)
        x0 = xi[0, rows].astype(F32)
        x1 = xi[1, rows].astype(F32)
        c = ctf[rows]
        scaled = c * weight
        twice = 2.0 * scaled
        left[rows, :k_dev] = (twice * x0).astype(BF16)
        left[rows, k_dev : 2 * k_dev] = (twice * x1).astype(BF16)
        left[rows, 2 * k_dev :] = (-scaled * c).astype(BF16)
        corr[rows, :k_dev] = (c * x0).astype(BF16)
        corr[rows, k_dev:] = (c * x1).astype(BF16)
        q2[rows] = x0 * x0 + x1 * x1
    for row in range(0, orient, 32):
        rows = slice(row, row + 32)
        prj[rows, :k_dev] = pi[0, rows]
        prj[rows, k_dev : 2 * k_dev] = pi[1, rows]
        p0 = pi[0, rows].astype(F32)
        p1 = pi[1, rows].astype(F32)
        prj[rows, 2 * k_dev :] = (p0 * p0 + p1 * p1).astype(BF16)
    part = matmul(left[...], prj[...], ((1,), (1,)))
    sig_pad = jnp.concatenate([sig_t[...], jnp.zeros((128 - n_sig, n_img), jnp.int32)], axis=0)
    index = sig_pad.T
    first = jnp.take_along_axis(part[:, :128], jnp.minimum(index, 127), axis=1)
    rest = jnp.concatenate([part[:, 128:], jnp.zeros((n_img, 256 - orient), F32)], axis=1)
    second = jnp.take_along_axis(rest, jnp.maximum(index - 128, 0), axis=1)
    picked = jnp.where(index < 128, first, second).T[:n_sig]
    short = n_sig // 2
    for n in range(NX):
        compact[n, :n_sig] = picked[:, :128]
        compact[n, n_sig : 2 * n_sig] = picked[:, 128:256]
        compact[n, 2 * n_sig :, :64] = picked[:short, 256:]
        compact[n, 2 * n_sig :, 64:] = picked[short:, 256:]


def relay_kernel(stack, out):
    total = (stack[0] + stack[2]) + (stack[1] + stack[3])
    for n in range(NZ):
        out[n] = total


def targets(me, orient, owned):
    my_h, my_c = me // (2 * NY), me % 2
    pos = lax.broadcasted_iota(jnp.int32, (orient, orient), 0)
    a = jnp.where(pos < orient // 2, 0, 1)
    h = pos - a * (orient // 2)
    d = jnp.where(h < 8 * NY, h >> 3, (h - 8 * NY) >> 2)
    q = jnp.where(h < 8 * NY, h & 7, 8 + (h & 3))
    b = jnp.where(q < owned, 0, 1)
    y = ((d & 1) << 2) + (d >> 1)
    owner = (((my_h + 1 - b) & 1) * NY + y) * 2 + ((my_c + 1 - a) & 1)
    return owner * owned + q - b * owned


def mid_kernel(stack, sig_t, corr, q2, prj, table, grp, total, away, mine):
    groups, k_dev = table.shape
    n_sig, n_img = sig_t.shape
    orient = prj.shape[0]
    half = orient // 2
    packed = (stack[0] + stack[2]) + (stack[1] + stack[3])
    last = packed[2 * n_sig :]
    scores = jnp.concatenate(
        [packed[:n_sig], packed[n_sig : 2 * n_sig], jnp.concatenate([last[:, :64], last[:, 64:]], axis=0)], axis=1
    )
    expo = jnp.exp(scores - jnp.max(scores, axis=0, keepdims=True))
    w_c = (expo / jnp.sum(expo, axis=0, keepdims=True)).astype(BF16).astype(F32)
    sig = sig_t[...].astype(F32).astype(BF16)
    w_b = w_c.astype(BF16)
    blocks = []
    for base in range(0, orient, 96):
        ids = (lax.broadcasted_iota(jnp.int32, (96, n_img), 0) + base).astype(F32).astype(BF16)
        acc = jnp.zeros((96, n_img), BF16)
        for s in range(n_sig):
            acc = jnp.where(sig[s : s + 1] == ids, w_b[s : s + 1], acc)
        blocks.append(acc)
    w_t = jnp.concatenate(blocks, axis=0)
    target = targets(lax.axis_index("img"), orient, orient // (4 * NY))
    shuffle = (target == lax.broadcasted_iota(jnp.int32, (orient, orient), 1)).astype(F32).astype(BF16)
    w_s = matmul(shuffle, w_t, ((1,), (0,))).astype(BF16)
    w_sum = matmul(w_t, jnp.ones((orient, 128), BF16), ((0,), (0,)))
    onehot = (grp[...][None, :] == lax.broadcasted_iota(jnp.int32, (groups, n_img), 0)).astype(F32).astype(BF16)
    w_g = matmul(onehot, w_t, ((1,), (1,)))
    away[:half] = matmul(w_s[:half], corr[...], ((1,), (0,)))
    mine[:half] = matmul(w_s[half:], corr[...], ((1,), (0,)))
    mix = matmul(thirds(w_g), prj[:, 2 * k_dev :], ((1,), (0,)))
    mix = (mix[:groups] + mix[groups : 2 * groups]) + mix[2 * groups :]
    noise = jnp.sum(table[...] * table[...] * mix, axis=0, keepdims=True)
    plain = [
        jnp.sum(q2[:, at : at + 128] * w_sum, axis=0, keepdims=True) for at in range(0, k_dev, 128)
    ]
    noise = noise + jnp.concatenate(plain, axis=1)
    for c in range(2):
        at = c * k_dev
        right = matmul(shuffle, prj[:, at : at + k_dev], ((1,), (0,)))
        cross = jnp.sum(right[:half] * away[:half, at : at + k_dev], axis=0, keepdims=True)
        cross = cross + jnp.sum(right[half:] * mine[:half, at : at + k_dev], axis=0, keepdims=True)
        noise = noise - 2.0 * cross
    noise = noise * (1.0 / total)
    e_half = exponent(away[:half])
    e_tail = exponent(noise)
    away[:half] = away[:half] * jnp.exp2(TOP - e_half)
    away[half:] = jnp.zeros((8, 2 * k_dev), F32)
    away[half : half + 1, :k_dev] = noise * jnp.exp2(TOP - e_tail)
    away[half : half + 1, k_dev : k_dev + 128] = jnp.broadcast_to(e_half, (1, 128))
    away[half : half + 1, k_dev + 128 :] = jnp.broadcast_to(e_tail, (1, k_dev - 128))
    mine[half:] = jnp.zeros((8, 2 * k_dev), F32)
    mine[half : half + 1, :k_dev] = noise


def pack_kernel(mine, got, chunks):
    half = mine.shape[0] - 8
    k_dev = mine.shape[1] // 2
    e_half = got[half : half + 1, k_dev : k_dev + 1]
    e_tail = got[half : half + 1, k_dev + 128 : k_dev + 129]
    data = mine[:half] + got[:half] * jnp.exp2(e_half - TOP)
    tail = mine[half : half + 1, :k_dev] + got[half : half + 1, :k_dev] * jnp.exp2(e_tail - TOP)
    e_half = exponent(data)
    e_tail = exponent(tail)
    data = data * jnp.exp2(TOP - e_half)
    tail = tail * jnp.exp2(TOP - e_tail)
    wide = k_dev // 5
    side = [tail[:, n * wide : (n + 1) * wide] for n in range(5)]
    side = side + [jnp.broadcast_to(v, (1, wide)) for v in (e_half, e_tail, e_tail)]
    side = jnp.concatenate(side, axis=0)
    for d in range(NY):
        chunks[d, :, : 2 * k_dev] = data[8 * d : 8 * d + 8]
        low = data[8 * NY + 4 * d : 8 * NY + 4 * d + 4]
        chunks[d, :4, 2 * k_dev : 3 * k_dev] = low[:, :k_dev]
        chunks[d, 4:, 2 * k_dev : 3 * k_dev] = low[:, k_dev:]
        chunks[d, :, 3 * k_dev :] = side


def sum_kernel(owned, chunks, send, keep, last):
    k_dev = last.shape[1]
    data = jnp.zeros((8, 3 * k_dev), F32)
    tail = jnp.zeros((8, k_dev // 5), F32)
    e_half = None
    for d in range(NY):
        side = chunks[d, :, 3 * k_dev :]
        one, two = side[5:6, :1], side[6:7, :1]
        data = data + chunks[d, :, : 3 * k_dev] * jnp.exp2(one - TOP)
        tail = tail + side * jnp.exp2(two - TOP)
        e_half = one if d == 0 else jnp.maximum(e_half, one)
        e_tail = two if d == 0 else jnp.maximum(e_tail, two)
    row = jnp.concatenate([tail[n : n + 1] for n in range(5)], axis=1)
    send[:owned] = data[:owned, : 2 * k_dev] * jnp.exp2(TOP - 3.0 - e_half)
    send[owned : owned + 1, :k_dev] = row * jnp.exp2(TOP - 3.0 - e_tail)
    send[owned : owned + 1, k_dev : k_dev + 128] = jnp.broadcast_to(e_half, (1, 128))
    send[owned : owned + 1, k_dev + 128 :] = jnp.broadcast_to(e_tail, (1, k_dev - 128))
    send[owned + 1 :] = jnp.zeros((7 - owned, 2 * k_dev), F32)
    left = 8 - owned
    for c in range(2):
        at = c * k_dev
        keep[:left, at : at + k_dev] = data[owned:, at : at + k_dev]
        keep[left:owned, at : at + k_dev] = data[4 * c : 4 * c + 4, 2 * k_dev : 3 * k_dev]
    keep[owned:] = jnp.zeros((8 - owned, 2 * k_dev), F32)
    last[...] = row


def end_kernel(owned, keep, last, got, slices, spectrum):
    k_dev = last.shape[1]
    grow = jnp.exp2(got[owned : owned + 1, k_dev : k_dev + 1] - (TOP - 3.0))
    grow_tail = jnp.exp2(got[owned : owned + 1, k_dev + 128 : k_dev + 129] - (TOP - 3.0))
    out = keep[:owned] + got[:owned] * grow
    for c in range(2):
        slices[:, c, :] = out[:, c * k_dev : (c + 1) * k_dev]
    spectrum[...] = (last[...] + got[owned : owned + 1, :k_dev] * grow_tail).reshape(k_dev)


VM = pl.BlockSpec(memory_space=pltpu.VMEM)


def call(body, ins, outs, scratch=()):
    return pl.pallas_call(
        body,
        in_specs=[VM] * ins,
        out_specs=[VM] * len(outs),
        out_shape=[jax.ShapeDtypeStruct(s, t) for s, t in outs],
        scratch_shapes=list(scratch),
        compiler_params=PARAMS,
    )


def spread(v, axis, groups=None):
    return lax.all_to_all(v, axis, 0, 0, axis_index_groups=groups, tiled=True)


def img_shift(v, dh, dc):
    perm = []
    for h in range(2):
        for y in range(NY):
            for c in range(2):
                to = (h + dh) % 2 * NY + y
                perm.append(((h * NY + y) * 2 + c, to * 2 + (c + dc) % 2))
    return lax.ppermute(v, "img", perm)


def pre(images, projections, ctf_table, grp, noise_weight, sig_t):
    n_img, _, k_dev = images.shape
    orient = projections.shape[0]
    packed = (NX, sig_t.shape[0] * n_img // 128, 128)
    return call(
        pre_kernel,
        6,
        [
            (packed, F32),
            ((n_img, 2 * k_dev), BF16),
            ((n_img, k_dev), F32),
            ((orient, 3 * k_dev), BF16),
        ],
        [pltpu.VMEM((n_img, 3 * k_dev), BF16), pltpu.VMEM((n_img, k_dev), F32)],
    )(
        images.transpose(1, 0, 2),
        projections.transpose(1, 0, 2),
        ctf_table,
        grp,
        noise_weight,
        sig_t,
    )


def mid(stack, sig_t, corr, q2, prj, ctf_table, grp, total):
    orient, k_dev = prj.shape[0], ctf_table.shape[1]

    def body(*refs):
        mid_kernel(*refs[:7], total, *refs[7:])

    shape = ((orient // 2 + 8, 2 * k_dev), F32)
    return call(body, 7, [shape, shape])(stack, sig_t, corr, q2, prj, ctf_table, grp)


def per_device(images, projections, ctf_table, ctf_group, noise_weight, significant):
    img_rows, _, k_dev = images.shape
    orient = projections.shape[0]
    owned = orient // lax.axis_size("img")
    total = img_rows * lax.axis_size("img")
    sig_t = significant.T
    compact, corr, q2, prj = pre(images, projections, ctf_table, ctf_group, noise_weight, sig_t)
    along_x = [[z * NX + x for x in FOUR] for z in range(NZ)]
    along_z = [[z * NX + x for z in FOUR] for x in range(NX)]
    compact = spread(compact, "blk", along_x)
    compact = call(relay_kernel, 1, [(compact.shape, F32)])(compact)[0]
    stack = spread(compact, "blk", along_z)
    away, mine = mid(stack, sig_t, corr, q2, prj, ctf_table, ctf_group, total)
    got = img_shift(away.astype(F16), 0, 1).astype(F32)
    shape = (8, 3 * k_dev + k_dev // 5)
    chunks = call(pack_kernel, 2, [((NY,) + shape, F32)])(mine, got)[0]
    along_y = [[(h * NY + y) * 2 + c for y in ORDER] for h in range(2) for c in range(2)]
    chunks = spread(chunks.astype(F16), "img", along_y).astype(F32)
    wide = (8, 2 * k_dev)

    def add(*refs):
        sum_kernel(owned, *refs)

    def end(*refs):
        end_kernel(owned, *refs)

    send, keep, last = call(add, 1, [(wide, F32), (wide, F32), ((1, k_dev), F32)])(chunks)
    got = img_shift(send.astype(F16), 1, 0).astype(F32)
    slices, spectrum = call(end, 3, [((owned, 2, k_dev), F32), ((k_dev,), F32)])(keep, last, got)
    return (slices, spectrum)


def solution(mesh):
    return jax.shard_map(
        per_device,
        mesh=mesh,
        in_specs=(
            P("img", None, "blk"),
            P(None, None, "blk"),
            P(None, "blk"),
            P("img"),
            P("blk"),
            P("img", None),
        ),
        out_specs=(P("img", None, "blk"), P("blk")),
        check_vma=False,
    )
```
